256 devices in a mesh: seq: 64 (over z, x, core), head: 4 (over y).
Axes of the slice: x: 4, y: 4, z: 8, core: 2. Of those that a mesh axis runs over, the one named last changes fastest.
Arguments:
- queries: bfloat16 [131072, 8, 128], P('seq', 'head'), may hold values from -12.5 to 12.5
- key_rows_all_heads: bfloat16 [131072, 8, 128], P('seq', 'head'), may hold values from -12.5 to 12.5
- values: bfloat16 [131072, 8, 128], P('seq', 'head'), may hold values from -24 to 24
- output_gain: float32 [8, 128], P('head'), may hold values from 0.1 to 1.9
Outputs:
- normed_output: bfloat16 [131072, 8, 128], P('seq', 'head')
The draws below stay inside these ranges and needn't reach their ends.
All inputs are finite; a program needn't handle non-finite values.
Results may differ from the reference program's by a relative error of at most 0.0087.
Values may be sent and summed in bfloat16 or wider, within the bound.
A program may use at most 64 MiB of HBM per device.

```python
import jax
import jax.numpy as jnp
from jax import lax

HEADS = 8
HEAD_DIM = 128
LANDMARKS = 512
NEWTON_STEPS = 2
TOKENS = 131072
SEGMENT = 256


def segment_parts(key):
    drawn_parts = jax.random.normal(key, (LANDMARKS, 1, HEADS, HEAD_DIM), jnp.float32)
    return jnp.clip(drawn_parts, -4.0, 4.0)


def spread_rows(segment_values):
    return jnp.broadcast_to(segment_values, (LANDMARKS, SEGMENT, HEADS, HEAD_DIM)).reshape(TOKENS, HEADS, HEAD_DIM)


def combine_rows(key, segment_values):
    noise = jnp.clip(jax.random.normal(key, (TOKENS, HEADS, HEAD_DIM), jnp.float32), -4.0, 4.0)
    return noise + spread_rows(segment_values)


def assemble(key, segment_values):
    return combine_rows(key, segment_values).astype(jnp.bfloat16)


def draw_queries(key, part):
    common = segment_parts(key)
    key = jax.random.fold_in(key, 3)
    return assemble(key, 0.8 * common)


def draw_key_rows_all_heads(key, part):
    common = segment_parts(key)
    key = jax.random.fold_in(key, 4)
    return assemble(key, 0.8 * common)


def draw_values(key, part):
    key = jax.random.fold_in(key, 7)
    segment_values = jnp.clip(jax.random.normal(jax.random.fold_in(key, 1), (LANDMARKS, 1, HEADS, HEAD_DIM), jnp.float32), -3.0, 3.0)
    noise = jnp.clip(jax.random.normal(key, (TOKENS, HEADS, HEAD_DIM), jnp.float32), -3.0, 3.0)
    ladder = jnp.arange(HEADS, dtype=jnp.float32) / (HEADS - 1)
    scales = 3.0 ** ladder
    return ((noise + spread_rows(segment_values)) * scales[None, :, None]).astype(jnp.bfloat16)


def setup_inputs(seed: int = 0) -> dict:
    splits = jax.random.split(jax.random.key(seed), 5)
    return {
        "queries": draw_queries(jax.random.fold_in(splits[4], 71), 0),
        "key_rows_all_heads": draw_key_rows_all_heads(jax.random.fold_in(splits[4], 71), 0),
        "values": draw_values(jax.random.fold_in(splits[4], 71), 0),
        "output_gain": jnp.clip(1.0 + 0.18 * jax.random.normal(splits[3], (HEADS, HEAD_DIM), jnp.float32), 0.1, 1.9),
    }


epsilon = 1e-06

def softmax_last(scores):
    row_top = lax.optimization_barrier(jnp.max(scores, axis=-1, keepdims=True))
    weights = jnp.exp(scores - row_top)
    return weights / lax.optimization_barrier(jnp.sum(weights, axis=-1, keepdims=True))

def landmark_means(head_tokens):
    summed = lax.optimization_barrier(jnp.sum(head_tokens.reshape(LANDMARKS, SEGMENT, HEAD_DIM), axis=1, dtype=jnp.float32))
    return (summed / SEGMENT).astype(jnp.bfloat16)

def full_product(first_factor, second_factor):
    return jnp.dot(first_factor, second_factor, precision=lax.Precision.HIGHEST)

def newton_inverse(matrix):
    identity = jnp.eye(LANDMARKS, dtype=jnp.float32)
    magnitude = jnp.abs(matrix)
    column_top = jnp.max(lax.optimization_barrier(jnp.sum(magnitude, axis=0)))
    row_top = jnp.max(lax.optimization_barrier(jnp.sum(magnitude, axis=1)))
    inverse = matrix.T / (column_top * row_top)
    for repeat in range(NEWTON_STEPS):
        product = full_product(matrix, inverse)
        nested = full_product(product, 7.0 * identity - product)
        nested = full_product(product, 15.0 * identity - nested)
        inverse = full_product(0.25 * inverse, 13.0 * identity - nested)
    return inverse

def reference(queries, key_rows_all_heads, values, output_gain):
    score_scale = HEAD_DIM ** (-0.5)

    def one_head(head_inputs):
        query_head, key_head, value_head = head_inputs
        query_landmark_rows = landmark_means(query_head)
        key_landmark_rows = landmark_means(key_head)
        scores_b = jnp.dot(query_landmark_rows, key_head.T, preferred_element_type=jnp.float32) * score_scale
        row_top = lax.optimization_barrier(jnp.max(scores_b, axis=-1, keepdims=True))
        landmark_weight_rows = jnp.exp(scores_b - row_top)
        total_b = lax.optimization_barrier(jnp.sum(landmark_weight_rows, axis=-1, keepdims=True))
        kernel_values = jnp.dot(landmark_weight_rows.astype(jnp.bfloat16), value_head, preferred_element_type=jnp.float32) / total_b
        landmark_kernel = softmax_last(jnp.dot(query_landmark_rows, key_landmark_rows.T, preferred_element_type=jnp.float32) * score_scale)
        inverse = newton_inverse(landmark_kernel)
        blended_value_rows = full_product(inverse, kernel_values).astype(jnp.bfloat16)
        scores_f = jnp.dot(query_head, key_landmark_rows.T, preferred_element_type=jnp.float32) * score_scale
        query_weight_rows = softmax_last(scores_f).astype(jnp.bfloat16)
        return jnp.dot(query_weight_rows, blended_value_rows, preferred_element_type=jnp.float32)
    attended = lax.map(one_head, (jnp.swapaxes(queries, 0, 1), jnp.swapaxes(key_rows_all_heads, 0, 1), jnp.swapaxes(values, 0, 1)))
    squares = lax.optimization_barrier(jnp.sum(attended * attended, axis=(0, 2)))
    factor = 1.0 / jnp.sqrt(squares / (HEADS * HEAD_DIM) + epsilon)
    normed = jnp.swapaxes(attended * factor[None, :, None], 0, 1) * output_gain[None]
    return normed.astype(jnp.bfloat16)
```

```python
import functools

import jax
import jax.numpy as jnp
from jax import lax
from jax.experimental import pallas as pl
from jax.experimental.pallas import tpu as pltpu
from jax.sharding import PartitionSpec as P

MESH = pl.DeviceIdType.MESH
F32 = jnp.float32
BF16 = jnp.bfloat16
NZ, NX, NC, NY = 8, 4, 2, 4
TOKENS = 2048
DIM = 128
MARKS = 512
SEGMENT = 256
EPSILON = 1e-06
LOG2E = 1.4426950408889634
SCALE2 = DIM ** (-0.5) * LOG2E

NN = (((1,), (0,)), ((), ()))
NT = (((1,), (1,)), ((), ()))


def dot(a, b, dims=NN):
    return lax.dot_general(a, b, dims, preferred_element_type=F32)


def split(a):
    high = a.astype(BF16)
    return high, (a - high.astype(F32)).astype(BF16)


def dot3(a, b, dims=NN):
    return dot(a[0], b[0], dims) + (dot(a[0], b[1], dims) + dot(a[1], b[0], dims))


def merge(values, tops):
    top = functools.reduce(jnp.maximum, tops)
    weights = [jnp.exp2(t - top) for t in tops]
    total = functools.reduce(jnp.add, weights)
    scale = 1.0 / total
    merged = functools.reduce(jnp.add, [v * (w * scale) for v, w in zip(values, weights)])
    return merged, top + jnp.log2(total)


def kernel(
    q_hbm, k_hbm, v_hbm, gain_ref, o_hbm,
    xq, xk, xv, qh, kh, vt, marks, gq, gk, mq, mk, wide,
    mine, away, rcore, xsum, rx, zsum, rz, kvt, kvf, weights_f,
    a_ref, t0, t1, t2, w_ref, mixt, att, sqs, sqr, out,
    local_sem, ssem, rsem,
):
    s = lax.axis_index("seq")
    y = lax.axis_index("head")
    c = lax.rem(s, 2)
    x = lax.rem(lax.div(s, 2), NX)
    z = lax.div(s, 2 * NX)
    other = 1 - c

    def at_z(d):
        zz = lax.rem(z + d, NZ)
        return {"seq": (zz * NX + x) * 2 + c}

    def at_x(d):
        xx = lax.rem(x + d, NX)
        return {"seq": (z * NX + xx) * 2 + c}

    sibling = {"seq": (z * NX + x) * 2 + other}

    def at_y(d):
        return {"head": lax.rem(y + d, NY)}

    counter = [0]
    started = []

    def send(src, dst, target):
        n = counter[0]
        counter[0] += 1
        copy = pltpu.make_async_remote_copy(
            src_ref=src, dst_ref=dst, send_sem=ssem.at[n], recv_sem=rsem.at[n],
            device_id=target, device_id_type=MESH,
        )
        copy.start()
        started.append(copy)
        return copy

    loads = [
        pltpu.make_async_copy(src, dst, local_sem.at[i])
        for i, (src, dst) in enumerate(((q_hbm, xq), (k_hbm, xk), (v_hbm, xv)))
    ]
    for load in loads:
        load.start()

    barrier = pltpu.get_barrier_semaphore()
    peers = [at_z(d) for d in range(1, NZ)] + [at_x(d) for d in range(1, NX)] + [sibling]
    peers += [at_y(d) for d in range(1, NY)]
    for peer in peers:
        pl.semaphore_signal(barrier, inc=1, device_id=peer, device_id_type=MESH)

    def means(src, dst):
        for j in range(TOKENS // SEGMENT):
            rows = src[pl.ds(j * 2 * SEGMENT, 2 * SEGMENT), :].astype(F32)
            total = jnp.sum(rows.reshape(2 * SEGMENT // 8, 8, DIM), axis=0)
            total = total + pltpu.roll(total, 4, 0)
            total = total + pltpu.roll(total, 2, 0)
            marks[j : j + 1, :] = total[0:1]
            marks[8 + j : 9 + j, :] = total[1:2]
        dst[c, x, z] = (marks[...] * (1.0 / SEGMENT)).astype(BF16)

    def gather_z(g):
        return [send(g.at[c, x, z], g.at[c, x, z], at_z(d)) for d in range(1, NZ)]

    def gather_x(g):
        return [send(g.at[c, x], g.at[c, x], at_x(d)) for d in range(1, NX)]

    def gather_core(g):
        return [send(g.at[c], g.at[c], sibling)]

    def arrived(copies):
        for copy in copies:
            copy.wait_recv()

    def head_rows(src, visit):
        def body(j, _):
            wide[...] = src[pl.ds(j * 512, 512), :].astype(F32)
            for h in range(2):
                visit(h, j, wide[pl.ds(h, 256, stride=2), :].astype(BF16))
            return 0

        lax.fori_loop(0, TOKENS // 256, body, 0)

    eye = (
        lax.broadcasted_iota(jnp.int32, (DIM, DIM), 0) == lax.broadcasted_iota(jnp.int32, (DIM, DIM), 1)
    ).astype(BF16)

    def keep_q(h, j, rows):
        qh[h, pl.ds(j * 256, 256), :] = rows

    def keep_k(h, j, rows):
        kh[h, pl.ds(j * 256, 256), :] = rows

    def keep_v(h, j, rows):
        vt[h, j] = dot(eye, rows, NT).astype(BF16)

    loads[0].wait()
    means(xq, gq)
    pl.semaphore_wait(barrier, len(peers))
    q_copies = gather_z(gq)
    loads[1].wait()
    means(xk, gk)
    k_copies = gather_z(gk)
    head_rows(xk, keep_k)
    arrived(q_copies)
    q_copies = gather_x(gq)
    arrived(k_copies)
    k_copies = gather_x(gk)
    loads[2].wait()
    head_rows(xv, keep_v)
    arrived(q_copies)
    q_copies = gather_core(gq)
    arrived(k_copies)
    k_copies = gather_core(gk)
    head_rows(xq, keep_q)
    arrived(q_copies)

    def landmarks(g, m):
        rows = g[...].astype(F32).reshape(NC * NX * NZ, 16, DIM)
        for h in range(2):
            m[h] = rows[:, 8 * h : 8 * h + 8, :].reshape(MARKS, DIM).astype(BF16)

    landmarks(gq, mq)

    def local_part(h, half, dst):
        scores = dot(kh[h], mq[h, pl.ds(half * 256, 256), :], NT)
        top = jnp.max(scores, axis=0, keepdims=True)
        weights = jnp.exp2((scores - top) * SCALE2)
        total = jnp.sum(weights, axis=0, keepdims=True)
        weights = weights.astype(BF16)
        part = dot(vt[h, 0], weights[0:256])
        for j in range(1, TOKENS // 256):
            part = part + dot(vt[h, j], weights[256 * j : 256 * j + 256])
        part = part * (1.0 / total)
        log_sum = top * SCALE2 + jnp.log2(total)
        for i in range(2):
            cut = slice(128 * i, 128 * i + 128)
            dst[2 * half + i, 0:DIM, :] = part[:, cut]
            dst[2 * half + i, DIM : DIM + 8, :] = jnp.broadcast_to(log_sum[:, cut], (8, 128))

    core_copies = []
    for half in range(2):
        local_part(other, half, away)
        cut = pl.ds(2 * half, 2)
        core_copies.append(send(away.at[cut], rcore.at[cut], sibling))
    for half in range(2):
        local_part(c, half, mine)

    for half in range(2):
        core_copies[half].wait_recv()
        for i in (2 * half, 2 * half + 1):
            value, log_sum = merge(
                [mine[i, 0:DIM, :], rcore[i, 0:DIM, :]],
                [mine[i, DIM : DIM + 1, :], rcore[i, DIM : DIM + 1, :]],
            )
            xsum[i, 0:DIM, :] = value
            xsum[i, DIM : DIM + 8, :] = jnp.broadcast_to(log_sum, (8, 128))
    x_copies = [send(xsum.at[lax.rem(x + d, NX)], rx.at[d - 1], at_x(d)) for d in range(1, NX)]

    arrived(k_copies)
    landmarks(gk, mk)
    scores = dot(mq[c], mk[c], NT)
    weights = jnp.exp2((scores - jnp.max(scores, axis=1, keepdims=True)) * SCALE2)
    a = weights * (1.0 / jnp.sum(weights, axis=1, keepdims=True))
    magnitude = jnp.abs(a)
    column_top = jnp.max(jnp.sum(magnitude, axis=0, keepdims=True), axis=1, keepdims=True)
    row_top = jnp.max(jnp.sum(magnitude, axis=1, keepdims=True), axis=0, keepdims=True)
    shrink = 1.0 / (column_top * row_top)
    a_ref[...] = a

    def eye_times(f):
        i = lax.broadcasted_iota(jnp.int32, (MARKS, MARKS), 0)
        j = lax.broadcasted_iota(jnp.int32, (MARKS, MARKS), 1)
        return jnp.where(i == j, F32(f), F32(0.0))

    a2 = split(a)
    t0[...] = dot3(a2, a2, NT) * shrink
    p0 = split(t0[...])
    t1[...] = dot3(p0, p0)

    arrived(x_copies)
    blocks = [xsum[x]] + [rx[d] for d in range(NX - 1)]
    value, log_sum = merge([b[0:DIM] for b in blocks], [b[DIM : DIM + 1] for b in blocks])
    log_sum = jnp.broadcast_to(log_sum, (8, 128))
    for i in range(NZ):
        zsum[i, 0:16, :] = value[16 * i : 16 * i + 16]
        zsum[i, 16:24, :] = log_sum
    z_copies = [send(zsum.at[lax.rem(z + d, NZ)], rz.at[d - 1], at_z(d)) for d in range(1, NZ)]

    s2 = split(t1[...])
    t2[...] = dot3(s2, p0)
    w_ref[...] = eye_times(13.0) - 15.0 * t0[...] + 7.0 * t1[...] - t2[...]
    t2[...] = 0.25 * dot3(p0, split(w_ref[...]))

    arrived(z_copies)
    blocks = [zsum[z]] + [rz[d] for d in range(NZ - 1)]
    value, _ = merge([b[0:16] for b in blocks], [b[16:17] for b in blocks])
    kvt[x, pl.ds(pl.multiple_of(16 * z, 16), 16), :] = value
    piece = kvt.at[x, pl.ds(pl.multiple_of(16 * z, 16), 16)]
    kv_copies = [send(piece, piece, at_z(d)) for d in range(1, NZ)]

    p1 = split(t2[...])
    t0[...] = dot3(p1, p1)
    t1[...] = eye_times(13.0) - 15.0 * t2[...] + dot3(split(t0[...]), split(eye_times(7.0) - t2[...]))

    arrived(kv_copies)
    kv_copies = [send(kvt.at[x], kvt.at[x], at_x(d)) for d in range(1, NX)]

    w_ref[...] = dot3(split(w_ref[...]), split(t1[...])) * (shrink * 0.0625)

    def query_weights(n, _):
        h = lax.div(n, TOKENS // 256)
        rows = pl.ds(pl.multiple_of(lax.rem(n, TOKENS // 256) * 256, 256), 256)
        scores = dot(qh[h, rows, :], mk[h], NT)
        weights = jnp.exp2((scores - jnp.max(scores, axis=1, keepdims=True)) * SCALE2)
        weights = weights * (1.0 / jnp.sum(weights, axis=1, keepdims=True))
        weights_f[h, rows, :] = weights.astype(BF16)
        return 0

    lax.fori_loop(0, 2 * TOKENS // 256, query_weights, 0)

    arrived(kv_copies)
    for i in range(NX):
        kvf[:, 128 * i : 128 * i + 128] = kvt[i]
    blended = dot3(split(kvf[...]), split(w_ref[...]))
    mixt[c] = dot3(split(blended), split(a_ref[...])).astype(BF16)
    mix_copy = send(mixt.at[c], mixt.at[c], sibling)

    def attend(h):
        def body(n, _):
            rows = pl.ds(pl.multiple_of(n * 256, 256), 256)
            att[h, rows, :] = dot(weights_f[h, rows, :], mixt[h], NT)
            return 0

        lax.fori_loop(0, TOKENS // 256, body, 0)

    attend(c)
    mix_copy.wait_recv()
    attend(other)

    ones = jnp.ones((8, DIM), BF16)
    for n in range(TOKENS // 256):
        rows = pl.ds(n * 256, 256)
        first, second = att[0, rows, :], att[1, rows, :]
        high, low = split(first * first + second * second)
        squares = dot(ones, high, NT) + dot(ones, low, NT)
        for i in range(2):
            sqs[2 * n + i : 2 * n + i + 1, :] = squares[0:1, 128 * i : 128 * i + 128]
    y_copies = [send(sqs, sqr.at[d - 1], at_y(d)) for d in range(1, NY)]
    arrived(y_copies)
    total = sqs[...] + sqr[0] + sqr[1] + sqr[2]
    sqs_factor = lax.rsqrt(total * (1.0 / (8 * DIM)) + EPSILON)

    stores = []
    for n in range(TOKENS // 128):
        rows = pl.ds(n * 128, 128)
        factor = jnp.broadcast_to(sqs_factor[n : n + 1, :], (DIM, DIM)).T
        for h in range(2):
            wide[pl.ds(h, 128, stride=2), :] = att[h, rows, :] * factor * gain_ref[h : h + 1, :]
        out[pl.ds(n * 256, 256), :] = wide[0:256, :].astype(BF16)
        if n % 4 == 3:
            cut = pl.ds((n - 3) * 256, 1024)
            store = pltpu.make_async_copy(out.at[cut], o_hbm.at[cut], local_sem.at[3 + n // 4])
            store.start()
            stores.append(store)
    for copy in started:
        copy.wait_send()
    for store in stores:
        store.wait()


def on_device(queries, key_rows, values, gain):
    rows = 2 * TOKENS
    args = [a.reshape(rows, DIM) for a in (queries, key_rows, values)]
    vmem = pltpu.VMEM
    out = pl.pallas_call(
        kernel,
        out_shape=jax.ShapeDtypeStruct((rows, DIM), BF16),
        in_specs=[pl.BlockSpec(memory_space=pl.ANY)] * 3 + [pl.BlockSpec(memory_space=pltpu.VMEM)],
        out_specs=pl.BlockSpec(memory_space=pl.ANY),
        scratch_shapes=[
            vmem((rows, DIM), BF16),
            vmem((rows, DIM), BF16),
            vmem((rows, DIM), BF16),
            vmem((2, TOKENS, DIM), BF16),
            vmem((2, TOKENS, DIM), BF16),
            vmem((2, TOKENS // 256, DIM, 256), BF16),
            vmem((16, DIM), F32),
            vmem((NC, NX, NZ, 16, DIM), BF16),
            vmem((NC, NX, NZ, 16, DIM), BF16),
            vmem((2, MARKS, DIM), BF16),
            vmem((2, MARKS, DIM), BF16),
            vmem((512, DIM), F32),
            vmem((NX, DIM + 8, DIM), F32),
            vmem((NX, DIM + 8, DIM), F32),
            vmem((NX, DIM + 8, DIM), F32),
            vmem((NX, DIM + 8, DIM), F32),
            vmem((NX - 1, DIM + 8, DIM), F32),
            vmem((NZ, 24, DIM), F32),
            vmem((NZ - 1, 24, DIM), F32),
            vmem((NX, DIM, DIM), F32),
            vmem((DIM, MARKS), F32),
            vmem((2, TOKENS, MARKS), BF16),
            vmem((MARKS, MARKS), F32),
            vmem((MARKS, MARKS), F32),
            vmem((MARKS, MARKS), F32),
            vmem((MARKS, MARKS), F32),
            vmem((MARKS, MARKS), F32),
            vmem((2, DIM, MARKS), BF16),
            vmem((2, TOKENS, DIM), F32),
            vmem((16, DIM), F32),
            vmem((NY - 1, 16, DIM), F32),
            vmem((rows, DIM), BF16),
            pltpu.SemaphoreType.DMA((8,)),
            pltpu.SemaphoreType.DMA((48,)),
            pltpu.SemaphoreType.DMA((48,)),
        ],
        compiler_params=pltpu.CompilerParams(
            collective_id=0, has_side_effects=True, vmem_limit_bytes=56 * 1024 * 1024
        ),
    )(*args, gain)
    return out.reshape(TOKENS, 2, DIM)


def solution(mesh):
    spec = P("seq", "head", None)
    return jax.shard_map(
        on_device,
        mesh=mesh,
        in_specs=(spec, spec, spec, P("head", None)),
        out_specs=spec,
        check_vma=False,
    )
```

```python
import jax
import jax.numpy as jnp
from jax import lax
from jax.experimental import pallas as pl
from jax.experimental.pallas import tpu as pltpu
from jax.sharding import PartitionSpec as P

MESH = pl.DeviceIdType.MESH
F32 = jnp.float32
BF16 = jnp.bfloat16
NZ, NX, NC, NY = 8, 4, 2, 4
TOKENS = 2048
DIM = 128
MARKS = 512
SEGMENT = 256
EPSILON = 1e-06
LOG2E = 1.4426950408889634
SCALE2 = DIM ** (-0.5) * LOG2E

NN = (((1,), (0,)), ((), ()))
NT = (((1,), (1,)), ((), ()))


def dot(a, b, dims=NN):
    return lax.dot_general(a, b, dims, preferred_element_type=F32)


def split(a):
    high = a.astype(BF16)
    return high, (a - high.astype(F32)).astype(BF16)


def dot3(a, b, dims=NN):
    return dot(a[0], b[0], dims) + (dot(a[0], b[1], dims) + dot(a[1], b[0], dims))


PEERS = sorted(
    ((dz, dx) for dz in range(NZ) for dx in range(NX) if dz or dx),
    key=lambda p: -(min(p[0], NZ - p[0]) + min(p[1], NX - p[1])),
)
NP = len(PEERS)


def kernel(
    q_hbm, k_hbm, v_hbm, gain_ref, o_hbm,
    xq, xk, xv, qh, kh, vh, marks, gq, gk, mq, mk, wide,
    away, rcore, parts, logs, rparts, rlogs, kvt, kvf, weights_f, totals,
    t0, t1, t2, w_ref, mixt, attt, att, sqs, sqr, out,
    local_sem, ssem, rsem,
):
    s = lax.axis_index("seq")
    y = lax.axis_index("head")
    c = lax.rem(s, 2)
    x = lax.rem(lax.div(s, 2), NX)
    z = lax.div(s, 2 * NX)
    other = 1 - c

    def at(d):
        return lax.rem(z + d[0], NZ), lax.rem(x + d[1], NX)

    def chip(d):
        zz, xx = at(d)
        return {"seq": (zz * NX + xx) * 2 + c}

    sibling = {"seq": (z * NX + x) * 2 + other}

    def at_y(d):
        return {"head": lax.rem(y + d, NY)}

    started = []

    def remote(src, dst, target, n):
        return pltpu.make_async_remote_copy(
            src_ref=src, dst_ref=dst, send_sem=ssem.at[n], recv_sem=rsem.at[n],
            device_id=target, device_id_type=MESH,
        )

    def send(src, dst, target):
        copy = remote(src, dst, target, len(started))
        copy.start()
        started.append(copy)
        return copy

    def send_all(pieces, size_of):
        n = len(started)
        for src, dst, d in pieces:
            remote(src, dst, chip(d), n).start()
        started.append(remote(size_of, size_of, sibling, n))
        return started[n]

    def arrived(copies):
        for copy in copies:
            copy.wait_recv()

    loads = [
        pltpu.make_async_copy(src, dst, local_sem.at[i])
        for i, (src, dst) in enumerate(((q_hbm, xq), (k_hbm, xk), (v_hbm, xv)))
    ]
    for load in loads:
        load.start()

    barrier = pltpu.get_barrier_semaphore()
    peers = [chip(d) for d in PEERS] + [sibling] + [at_y(d) for d in range(1, NY)]
    for peer in peers:
        pl.semaphore_signal(barrier, inc=1, device_id=peer, device_id_type=MESH)

    def means(src, dst):
        for j in range(TOKENS // SEGMENT):
            rows = src[pl.ds(j * 2 * SEGMENT, 2 * SEGMENT), :].astype(F32)
            total = jnp.sum(rows.reshape(2 * SEGMENT // 8, 8, DIM), axis=0)
            total = total + pltpu.roll(total, 4, 0)
            total = total + pltpu.roll(total, 2, 0)
            marks[j : j + 1, :] = total[0:1]
            marks[8 + j : 9 + j, :] = total[1:2]
        dst[c, x, z] = (marks[...] * (1.0 / SEGMENT)).astype(BF16)

    def spread(block):
        return [send_all([(block, block, d) for d in PEERS], rparts)]

    def head_rows(src, dst):
        def body(j, _):
            wide[0:512, :] = src[pl.ds(j * 512, 512), :].astype(F32)
            for h in range(2):
                dst[h, pl.ds(j * 256, 256), :] = wide[pl.ds(h, 256, stride=2), :].astype(BF16)
            return 0

        lax.fori_loop(0, TOKENS // 256, body, 0)

    def landmarks(g, m, core):
        rows = g[core].astype(F32).reshape(NX * NZ, 16, DIM)
        for h in range(2):
            m[h, core] = rows[:, 8 * h : 8 * h + 8, :].reshape(MARKS // 2, DIM).astype(BF16)

    loads[0].wait()
    means(xq, gq)
    pl.semaphore_wait(barrier, len(peers))
    q_copies = spread(gq.at[c, x, z])
    loads[1].wait()
    means(xk, gk)
    k_copies = spread(gk.at[c, x, z])
    head_rows(xk, kh)
    loads[2].wait()
    head_rows(xv, vh)
    head_rows(xq, qh)
    arrived(q_copies)
    q_copies = [send(gq.at[c], gq.at[c], sibling)]
    landmarks(gq, mq, c)

    def local_part(h, rows):
        scores = dot(rows, kh[h], NT)
        top = jnp.max(scores, axis=1, keepdims=True)
        weights = jnp.exp2((scores - top) * SCALE2)
        total = jnp.sum(weights, axis=1, keepdims=True)
        part = dot(weights.astype(BF16), vh[h]) * (1.0 / total)
        return part, jnp.broadcast_to(top * SCALE2 + jnp.log2(total), part.shape)

    core_copies = []

    def part_away(half):
        away[half, 0], away[half, 1] = local_part(other, mq[other, half])
        core_copies.append(send(away.at[half], rcore.at[half], sibling))

    part_away(c)
    arrived(q_copies)
    landmarks(gq, mq, other)
    part_away(other)
    arrived(k_copies)
    k_copies = [send(gk.at[c], gk.at[c], sibling)]
    value, log_sum = local_part(c, mq[c].reshape(MARKS, DIM))
    arrived(core_copies)
    far = jnp.concatenate([rcore[0, 0], rcore[1, 0]], axis=0)
    far_log = jnp.concatenate([rcore[0, 1], rcore[1, 1]], axis=0)
    top = jnp.maximum(log_sum, far_log)
    near_weight, far_weight = jnp.exp2(log_sum - top), jnp.exp2(far_log - top)
    total = near_weight + far_weight
    value = (value * near_weight + far * far_weight) * (1.0 / total)
    log_sum = top + jnp.log2(total)
    for i in range(NX):
        cut = slice(128 * i, 128 * i + 128)
        parts[i] = value[cut].T.astype(BF16).reshape(NZ, 16, DIM)
        logs[i] = log_sum[cut].T[0:1]
    log_pieces = [(logs.at[at(d)[1]], rlogs.at[n], d) for n, d in enumerate(PEERS)]
    part_pieces = [(parts.at[at(d)[1], at(d)[0]], rparts.at[n], d) for n, d in enumerate(PEERS)]
    reduce_copies = [send_all(log_pieces, rlogs), send_all(part_pieces, rparts)]

    arrived(k_copies)
    for core in range(2):
        landmarks(gk, mk, core)
    scores = dot(mq[c].reshape(MARKS, DIM), mk[c].reshape(MARKS, DIM), NT)
    weights = jnp.exp2((scores - jnp.max(scores, axis=1, keepdims=True)) * SCALE2)
    a = weights * (1.0 / jnp.sum(weights, axis=1, keepdims=True))
    magnitude = jnp.abs(a)
    column_top = jnp.max(jnp.sum(magnitude, axis=0, keepdims=True), axis=1, keepdims=True)
    row_top = jnp.max(jnp.sum(magnitude, axis=1, keepdims=True), axis=0, keepdims=True)
    shrink = 1.0 / (column_top * row_top)

    def eye_times(f):
        i = lax.broadcasted_iota(jnp.int32, (MARKS, MARKS), 0)
        j = lax.broadcasted_iota(jnp.int32, (MARKS, MARKS), 1)
        return jnp.where(i == j, F32(f), F32(0.0))

    a2 = split(a)
    t0[...] = dot3(a2, a2, NT) * shrink
    p0 = split(t0[...])
    t1[...] = dot3(p0, p0)
    s2 = split(t1[...])
    t2[...] = dot3(s2, p0)
    w_ref[...] = eye_times(13.0) - 15.0 * t0[...] + 7.0 * t1[...] - t2[...]
    t2[...] = 0.25 * dot3(p0, split(w_ref[...]))
    p1 = split(t2[...])
    t0[...] = dot3(p1, p1)

    arrived(reduce_copies)
    own_log, far_logs = logs[x], rlogs[...]
    top = jnp.maximum(own_log, jnp.max(far_logs, axis=0))
    own_weight, far_weights = jnp.exp2(own_log - top), jnp.exp2(far_logs - top[None])
    total = own_weight + jnp.sum(far_weights, axis=0)
    value = parts[x, z].astype(F32) * own_weight + jnp.sum(rparts[...].astype(F32) * far_weights, axis=0)
    kvt[x, z] = (value * (1.0 / total)).astype(BF16)
    kv_copies = spread(kvt.at[x, z])

    t1[...] = eye_times(13.0) - 15.0 * t2[...] + dot3(split(t0[...]), split(eye_times(7.0) - t2[...]))
    w_ref[...] = dot3(split(w_ref[...]), split(t1[...])) * (shrink * 0.0625)

    def query_weights(h, _):
        scores = dot(mk[h].reshape(MARKS, DIM), qh[h], NT)
        weights = jnp.exp2((scores - jnp.max(scores, axis=0, keepdims=True)) * SCALE2)
        totals[h] = jnp.sum(weights, axis=0, keepdims=True)
        weights_f[h] = weights.astype(BF16)
        return 0

    lax.fori_loop(0, 2, query_weights, 0)

    arrived(kv_copies)
    for i in range(NX):
        kvf[:, 128 * i : 128 * i + 128] = kvt[i].reshape(DIM, DIM)
    w2 = split(w_ref[...])
    blended = dot(kvf[...], w2[0]) + dot(kvf[...], w2[1])
    mixt[c] = dot3(split(blended), a2).astype(BF16)
    mix_copy = send(mixt.at[c], mixt.at[c], sibling)

    def attend(h):
        value = dot(mixt[h], weights_f[h]) * (1.0 / totals[h])
        attt[h] = value
        return jnp.sum(value * value, axis=0, keepdims=True)

    squares = attend(c)
    arrived([mix_copy])
    squares = squares + attend(other)
    for n in range(TOKENS // 128):
        sqs[n : n + 1, :] = squares[:, 128 * n : 128 * n + 128]
    y_copies = [send(sqs, sqr.at[d - 1], at_y(d)) for d in (2, 1, 3)]
    for n in range(TOKENS // 128):
        for h in range(2):
            att[h, pl.ds(n * 128, 128), :] = attt[h, :, 128 * n : 128 * n + 128].T * gain_ref[h : h + 1, :]
    arrived(y_copies)
    total = sqs[...] + sqr[0] + sqr[1] + sqr[2]
    factors = lax.rsqrt(total * (1.0 / (8 * DIM)) + EPSILON)

    stores = []
    for n in range(TOKENS // 128):
        rows = pl.ds(n * 128, 128)
        factor = jnp.broadcast_to(factors[n : n + 1, :], (DIM, DIM)).T
        for h in range(2):
            wide[pl.ds(n * 256 + h, 128, stride=2), :] = att[h, rows, :] * factor
        cut = pl.ds(n * 256, 256)
        out[cut, :] = wide[cut, :].astype(BF16)
        if n % 4 == 3:
            cut = pl.ds((n - 3) * 256, 1024)
            store = pltpu.make_async_copy(out.at[cut], o_hbm.at[cut], local_sem.at[3 + n // 4])
            store.start()
            stores.append(store)
    for copy in started:
        copy.wait_send()
    for store in stores:
        store.wait()


def on_device(queries, key_rows, values, gain):
    rows = 2 * TOKENS
    args = [a.reshape(rows, DIM) for a in (queries, key_rows, values)]
    vmem = pltpu.VMEM
    out = pl.pallas_call(
        kernel,
        out_shape=jax.ShapeDtypeStruct((rows, DIM), BF16),
        in_specs=[pl.BlockSpec(memory_space=pl.ANY)] * 3 + [pl.BlockSpec(memory_space=pltpu.VMEM)],
        out_specs=pl.BlockSpec(memory_space=pl.ANY),
        scratch_shapes=[
            vmem((rows, DIM), BF16),
            vmem((rows, DIM), BF16),
            vmem((rows, DIM), BF16),
            vmem((2, TOKENS, DIM), BF16),
            vmem((2, TOKENS, DIM), BF16),
            vmem((2, TOKENS, DIM), BF16),
            vmem((16, DIM), F32),
            vmem((NC, NX, NZ, 16, DIM), BF16),
            vmem((NC, NX, NZ, 16, DIM), BF16),
            vmem((2, 2, MARKS // 2, DIM), BF16),
            vmem((2, 2, MARKS // 2, DIM), BF16),
            vmem((rows, DIM), F32),
            vmem((2, 2, MARKS // 2, DIM), F32),
            vmem((2, 2, MARKS // 2, DIM), F32),
            vmem((NX, NZ, 16, DIM), BF16),
            vmem((NX, 1, DIM), F32),
            vmem((NP, 16, DIM), BF16),
            vmem((NP, 1, DIM), F32),
            vmem((NX, NZ, 16, DIM), BF16),
            vmem((DIM, MARKS), BF16),
            vmem((2, MARKS, TOKENS), BF16),
            vmem((2, 1, TOKENS), F32),
            vmem((MARKS, MARKS), F32),
            vmem((MARKS, MARKS), F32),
            vmem((MARKS, MARKS), F32),
            vmem((MARKS, MARKS), F32),
            vmem((2, DIM, MARKS), BF16),
            vmem((2, DIM, TOKENS), F32),
            vmem((2, TOKENS, DIM), F32),
            vmem((16, DIM), F32),
            vmem((NY - 1, 16, DIM), F32),
            vmem((rows, DIM), BF16),
            pltpu.SemaphoreType.DMA((7,)),
            pltpu.SemaphoreType.DMA((13,)),
            pltpu.SemaphoreType.DMA((13,)),
        ],
        compiler_params=pltpu.CompilerParams(
            collective_id=0, has_side_effects=True, vmem_limit_bytes=56 * 1024 * 1024
        ),
    )(*args, gain)
    return out.reshape(TOKENS, 2, DIM)


def solution(mesh):
    spec = P("seq", "head", None)
    return jax.shard_map(
        on_device,
        mesh=mesh,
        in_specs=(spec, spec, spec, P("head", None)),
        out_specs=spec,
        check_vma=False,
    )
```

```python
import jax
import jax.numpy as jnp
from jax import lax
from jax.experimental import pallas as pl
from jax.experimental.pallas import tpu as pltpu
from jax.sharding import PartitionSpec as P

MESH = pl.DeviceIdType.MESH
F32 = jnp.float32
BF16 = jnp.bfloat16
NZ, NX, NC, NY = 8, 4, 2, 4
TOKENS = 2048
DIM = 128
MARKS = 512
SEGMENT = 256
EPSILON = 1e-06
LOG2E = 1.4426950408889634
SCALE2 = DIM ** (-0.5) * LOG2E

NN = (((1,), (0,)), ((), ()))
NT = (((1,), (1,)), ((), ()))


def dot(a, b, dims=NN):
    return lax.dot_general(a, b, dims, preferred_element_type=F32)


def split(a):
    high = a.astype(BF16)
    return high, (a - high.astype(F32)).astype(BF16)


def dot3(a, b, dims=NN):
    return dot(a[0], b[0], dims) + (dot(a[0], b[1], dims) + dot(a[1], b[0], dims))


PEERS = sorted(
    ((dz, dx) for dz in range(NZ) for dx in range(NX) if dz or dx),
    key=lambda p: -(min(p[0], NZ - p[0]) + min(p[1], NX - p[1])),
)
NP = len(PEERS)


def kernel(
    q_hbm, k_hbm, v_hbm, gain_ref, o_hbm,
    xq, xk, xv, qh, kh, vh, marks, gq, gk, mq, mk, wide,
    away, rcore, parts, logs, rparts, rlogs, kvt, kvf, weights_f, totals,
    t0, t1, t2, w_ref, mixt, attt, att, sqs, sqr, out,
    local_sem, ssem, rsem,
):
    s = lax.axis_index("seq")
    y = lax.axis_index("head")
    c = lax.rem(s, 2)
    x = lax.rem(lax.div(s, 2), NX)
    z = lax.div(s, 2 * NX)
    other = 1 - c

    def at(d):
        return lax.rem(z + d[0], NZ), lax.rem(x + d[1], NX)

    def chip(d):
        zz, xx = at(d)
        return {"seq": (zz * NX + xx) * 2 + c}

    sibling = {"seq": (z * NX + x) * 2 + other}

    def at_y(d):
        return {"head": lax.rem(y + d, NY)}

    started = []

    def remote(src, dst, target, n):
        return pltpu.make_async_remote_copy(
            src_ref=src, dst_ref=dst, send_sem=ssem.at[n], recv_sem=rsem.at[n],
            device_id=target, device_id_type=MESH,
        )

    def send(src, dst, target):
        copy = remote(src, dst, target, len(started))
        copy.start()
        started.append(copy)
        return copy

    def send_all(pieces, size_of):
        n = len(started)
        for src, dst, d in pieces:
            remote(src, dst, chip(d), n).start()
        started.append(remote(size_of, size_of, sibling, n))
        return started[n]

    def arrived(copies):
        for copy in copies:
            copy.wait_recv()

    loads = [
        pltpu.make_async_copy(src, dst, local_sem.at[i])
        for i, (src, dst) in enumerate(((q_hbm, xq), (k_hbm, xk), (v_hbm, xv)))
    ]
    for load in loads:
        load.start()

    barrier = pltpu.get_barrier_semaphore()
    peers = [chip(d) for d in PEERS] + [sibling] + [at_y(d) for d in range(1, NY)]
    for peer in peers:
        pl.semaphore_signal(barrier, inc=1, device_id=peer, device_id_type=MESH)

    def means(src, dst):
        for j in range(TOKENS // SEGMENT):
            rows = src[pl.ds(j * 2 * SEGMENT, 2 * SEGMENT), :].astype(F32)
            total = jnp.sum(rows.reshape(2 * SEGMENT // 8, 8, DIM), axis=0)
            total = total + pltpu.roll(total, 4, 0)
            total = total + pltpu.roll(total, 2, 0)
            marks[j : j + 1, :] = total[0:1]
            marks[8 + j : 9 + j, :] = total[1:2]
        dst[c, x, z] = (marks[...] * (1.0 / SEGMENT)).astype(BF16)

    def spread(block):
        return [send_all([(block, block, d) for d in PEERS], rparts)]

    def head_rows(src, dst):
        def body(j, _):
            wide[0:512, :] = src[pl.ds(j * 512, 512), :].astype(F32)
            for h in range(2):
                dst[h, pl.ds(j * 256, 256), :] = wide[pl.ds(h, 256, stride=2), :].astype(BF16)
            return 0

        lax.fori_loop(0, TOKENS // 256, body, 0)

    def landmarks(g, m, core):
        rows = g[core].astype(F32).reshape(NX * NZ, 16, DIM)
        for h in range(2):
            m[h, core] = rows[:, 8 * h : 8 * h + 8, :].reshape(MARKS // 2, DIM).astype(BF16)

    loads[0].wait()
    means(xq, gq)
    pl.semaphore_wait(barrier, len(peers))
    q_copies = spread(gq.at[c, x, z])
    loads[1].wait()
    means(xk, gk)
    k_copies = spread(gk.at[c, x, z])
    head_rows(xk, kh)
    loads[2].wait()
    head_rows(xv, vh)
    head_rows(xq, qh)
    arrived(q_copies)
    q_copies = [send(gq.at[c], gq.at[c], sibling)]
    landmarks(gq, mq, c)

    def local_part(h, rows):
        scores = dot(rows, kh[h], NT)
        top = jnp.max(scores, axis=1, keepdims=True)
        weights = jnp.exp2((scores - top) * SCALE2)
        total = jnp.sum(weights, axis=1, keepdims=True)
        part = dot(weights.astype(BF16), vh[h]) * (1.0 / total)
        return part, jnp.broadcast_to(top * SCALE2 + jnp.log2(total), part.shape)

    core_copies = []

    def part_away(half):
        away[half, 0], away[half, 1] = local_part(other, mq[other, half])
        core_copies.append(send(away.at[half], rcore.at[half], sibling))

    part_away(c)
    arrived(q_copies)
    landmarks(gq, mq, other)
    part_away(other)
    arrived(k_copies)
    k_copies = [send(gk.at[c], gk.at[c], sibling)]
    value, log_sum = local_part(c, mq[c].reshape(MARKS, DIM))
    arrived(core_copies)
    far = jnp.concatenate([rcore[0, 0], rcore[1, 0]], axis=0)
    far_log = jnp.concatenate([rcore[0, 1], rcore[1, 1]], axis=0)
    top = jnp.maximum(log_sum, far_log)
    near_weight, far_weight = jnp.exp2(log_sum - top), jnp.exp2(far_log - top)
    total = near_weight + far_weight
    value = (value * near_weight + far * far_weight) * (1.0 / total)
    log_sum = top + jnp.log2(total)
    for i in range(NX):
        cut = slice(128 * i, 128 * i + 128)
        parts[i] = value[cut].T.astype(BF16).reshape(NZ, 16, DIM)
        logs[i] = log_sum[cut].T[0:1]
    log_pieces = [(logs.at[at(d)[1]], rlogs.at[n], d) for n, d in enumerate(PEERS)]
    part_pieces = [(parts.at[at(d)[1], at(d)[0]], rparts.at[n], d) for n, d in enumerate(PEERS)]
    reduce_copies = [send_all(log_pieces, rlogs), send_all(part_pieces, rparts)]

    arrived(k_copies)
    for core in range(2):
        landmarks(gk, mk, core)
    scores = dot(mq[c].reshape(MARKS, DIM), mk[c].reshape(MARKS, DIM), NT)
    weights = jnp.exp2((scores - jnp.max(scores, axis=1, keepdims=True)) * SCALE2)
    a = weights * (1.0 / jnp.sum(weights, axis=1, keepdims=True))
    magnitude = jnp.abs(a)
    column_top = jnp.max(jnp.sum(magnitude, axis=0, keepdims=True), axis=1, keepdims=True)
    row_top = jnp.max(jnp.sum(magnitude, axis=1, keepdims=True), axis=0, keepdims=True)
    shrink = 1.0 / (column_top * row_top)

    def eye_times(f):
        i = lax.broadcasted_iota(jnp.int32, (MARKS, MARKS), 0)
        j = lax.broadcasted_iota(jnp.int32, (MARKS, MARKS), 1)
        return jnp.where(i == j, F32(f), F32(0.0))

    a2 = split(a)
    t0[...] = dot3(a2, a2, NT) * shrink
    p0 = split(t0[...])
    t1[...] = dot3(p0, p0)
    cube = dot(t1[...].astype(BF16), p0[0])
    w_ref[...] = eye_times(13.0) - 15.0 * t0[...] + 7.0 * t1[...] - cube
    t2[...] = 0.25 * dot3(p0, split(w_ref[...]))

    arrived(reduce_copies)
    own_log, far_logs = logs[x], rlogs[...]
    top = jnp.maximum(own_log, jnp.max(far_logs, axis=0))
    own_weight, far_weights = jnp.exp2(own_log - top), jnp.exp2(far_logs - top[None])
    total = own_weight + jnp.sum(far_weights, axis=0)
    value = parts[x, z].astype(F32) * own_weight + jnp.sum(rparts[...].astype(F32) * far_weights, axis=0)
    kvt[x, z] = (value * (1.0 / total)).astype(BF16)
    kv_copies = spread(kvt.at[x, z])

    p1 = split(t2[...])
    t0[...] = dot3(p1, p1)
    cube = dot(t0[...].astype(BF16), p1[0])
    t1[...] = eye_times(13.0) - 15.0 * t2[...] + 7.0 * t0[...] - cube
    w_ref[...] = dot3(split(w_ref[...]), split(t1[...])) * (shrink * 0.0625)

    def query_weights(h, _):
        scores = dot(mk[h].reshape(MARKS, DIM), qh[h], NT)
        weights = jnp.exp2((scores - jnp.max(scores, axis=0, keepdims=True)) * SCALE2)
        totals[h] = jnp.sum(weights, axis=0, keepdims=True)
        weights_f[h] = weights.astype(BF16)
        return 0

    lax.fori_loop(0, 2, query_weights, 0)

    arrived(kv_copies)
    for i in range(NX):
        kvf[:, 128 * i : 128 * i + 128] = kvt[i].reshape(DIM, DIM)
    w2 = split(w_ref[...])
    blended = dot(kvf[...], w2[0]) + dot(kvf[...], w2[1])
    mixt[c] = dot3(split(blended), a2).astype(BF16)
    mix_copy = send(mixt.at[c], mixt.at[c], sibling)

    def attend(h):
        value = dot(mixt[h], weights_f[h]) * (1.0 / totals[h])
        attt[h] = value
        return jnp.sum(value * value, axis=0, keepdims=True)

    squares = attend(c)
    arrived([mix_copy])
    squares = squares + attend(other)
    for n in range(TOKENS // 128):
        sqs[n : n + 1, :] = squares[:, 128 * n : 128 * n + 128]
    y_copies = [send(sqs, sqr.at[d - 1], at_y(d)) for d in (2, 1, 3)]
    for n in range(TOKENS // 128):
        for h in range(2):
            att[h, pl.ds(n * 128, 128), :] = attt[h, :, 128 * n : 128 * n + 128].T * gain_ref[h : h + 1, :]
    arrived(y_copies)
    total = sqs[...] + sqr[0] + sqr[1] + sqr[2]
    factors = lax.rsqrt(total * (1.0 / (8 * DIM)) + EPSILON)

    stores = []
    for n in range(TOKENS // 128):
        rows = pl.ds(n * 128, 128)
        factor = jnp.broadcast_to(factors[n : n + 1, :], (DIM, DIM)).T
        for h in range(2):
            wide[pl.ds(n * 256 + h, 128, stride=2), :] = att[h, rows, :] * factor
        cut = pl.ds(n * 256, 256)
        out[cut, :] = wide[cut, :].astype(BF16)
        if n % 4 == 3:
            cut = pl.ds((n - 3) * 256, 1024)
            store = pltpu.make_async_copy(out.at[cut], o_hbm.at[cut], local_sem.at[3 + n // 4])
            store.start()
            stores.append(store)
    for copy in started:
        copy.wait_send()
    for store in stores:
        store.wait()


def on_device(queries, key_rows, values, gain):
    rows = 2 * TOKENS
    args = [a.reshape(rows, DIM) for a in (queries, key_rows, values)]
    vmem = pltpu.VMEM
    out = pl.pallas_call(
        kernel,
        out_shape=jax.ShapeDtypeStruct((rows, DIM), BF16),
        in_specs=[pl.BlockSpec(memory_space=pl.ANY)] * 3 + [pl.BlockSpec(memory_space=pltpu.VMEM)],
        out_specs=pl.BlockSpec(memory_space=pl.ANY),
        scratch_shapes=[
            vmem((rows, DIM), BF16),
            vmem((rows, DIM), BF16),
            vmem((rows, DIM), BF16),
            vmem((2, TOKENS, DIM), BF16),
            vmem((2, TOKENS, DIM), BF16),
            vmem((2, TOKENS, DIM), BF16),
            vmem((16, DIM), F32),
            vmem((NC, NX, NZ, 16, DIM), BF16),
            vmem((NC, NX, NZ, 16, DIM), BF16),
            vmem((2, 2, MARKS // 2, DIM), BF16),
            vmem((2, 2, MARKS // 2, DIM), BF16),
            vmem((rows, DIM), F32),
            vmem((2, 2, MARKS // 2, DIM), F32),
            vmem((2, 2, MARKS // 2, DIM), F32),
            vmem((NX, NZ, 16, DIM), BF16),
            vmem((NX, 1, DIM), F32),
            vmem((NP, 16, DIM), BF16),
            vmem((NP, 1, DIM), F32),
            vmem((NX, NZ, 16, DIM), BF16),
            vmem((DIM, MARKS), BF16),
            vmem((2, MARKS, TOKENS), BF16),
            vmem((2, 1, TOKENS), F32),
            vmem((MARKS, MARKS), F32),
            vmem((MARKS, MARKS), F32),
            vmem((MARKS, MARKS), F32),
            vmem((MARKS, MARKS), F32),
            vmem((2, DIM, MARKS), BF16),
            vmem((2, DIM, TOKENS), F32),
            vmem((2, TOKENS, DIM), F32),
            vmem((16, DIM), F32),
            vmem((NY - 1, 16, DIM), F32),
            vmem((rows, DIM), BF16),
            pltpu.SemaphoreType.DMA((7,)),
            pltpu.SemaphoreType.DMA((13,)),
            pltpu.SemaphoreType.DMA((13,)),
        ],
        compiler_params=pltpu.CompilerParams(
            collective_id=0, has_side_effects=True, vmem_limit_bytes=56 * 1024 * 1024
        ),
    )(*args, gain)
    return out.reshape(TOKENS, 2, DIM)


def solution(mesh):
    spec = P("seq", "head", None)
    return jax.shard_map(
        on_device,
        mesh=mesh,
        in_specs=(spec, spec, spec, P("head", None)),
        out_specs=spec,
        check_vma=False,
    )
```

```python
import functools

import jax
import jax.numpy as jnp
from jax import lax
from jax.experimental import pallas as pl
from jax.experimental.pallas import tpu as pltpu
from jax.sharding import PartitionSpec as P

MESH = pl.DeviceIdType.MESH
F32 = jnp.float32
BF16 = jnp.bfloat16
NZ, NX, NC, NY = 8, 4, 2, 4
TOKENS = 2048
DIM = 128
MARKS = 512
SEGMENT = 256
EPSILON = 1e-06
LOG2E = 1.4426950408889634
SCALE2 = DIM ** (-0.5) * LOG2E

NN = (((1,), (0,)), ((), ()))
NT = (((1,), (1,)), ((), ()))


def dot(a, b, dims=NN):
    return lax.dot_general(a, b, dims, preferred_element_type=F32)


def split(a):
    high = a.astype(BF16)
    return high, (a - high.astype(F32)).astype(BF16)


def dot3(a, b, dims=NN):
    return dot(a[0], b[0], dims) + (dot(a[0], b[1], dims) + dot(a[1], b[0], dims))


PEERS = sorted(
    ((dz, dx) for dz in range(NZ) for dx in range(NX) if dz or dx),
    key=lambda p: -(min(p[0], NZ - p[0]) + min(p[1], NX - p[1])),
)
NP = len(PEERS)


def kernel(
    q_hbm, k_hbm, v_hbm, gain_hbm, att, factors,
    xq, xk, xv, gain_ref, qh, kh, vh, marks, gq, gk, mq, mk, wide,
    away, rcore, parts, logs, rparts, rlogs, kvt, kvf, weights_f, totals,
    t0, t1, t2, w_ref, mixt, attt, sqs, sqr,
    local_sem, ssem, rsem,
):
    s = lax.axis_index("seq")
    y = lax.axis_index("head")
    c = lax.rem(s, 2)
    x = lax.rem(lax.div(s, 2), NX)
    z = lax.div(s, 2 * NX)
    other = 1 - c

    def at(d):
        return lax.rem(z + d[0], NZ), lax.rem(x + d[1], NX)

    def chip(d):
        zz, xx = at(d)
        return {"seq": (zz * NX + xx) * 2 + c}

    sibling = {"seq": (z * NX + x) * 2 + other}

    def at_y(d):
        return {"head": lax.rem(y + d, NY)}

    started = []

    def remote(src, dst, target, n):
        return pltpu.make_async_remote_copy(
            src_ref=src, dst_ref=dst, send_sem=ssem.at[n], recv_sem=rsem.at[n],
            device_id=target, device_id_type=MESH,
        )

    def send(src, dst, target):
        copy = remote(src, dst, target, len(started))
        copy.start()
        started.append(copy)
        return copy

    def send_all(pieces, size_of):
        n = len(started)
        for src, dst, d in pieces:
            remote(src, dst, chip(d), n).start()
        started.append(remote(size_of, size_of, sibling, n))
        return started[n]

    def arrived(copies):
        for copy in copies:
            copy.wait_recv()

    loads = [
        pltpu.make_async_copy(src, dst, local_sem.at[i])
        for i, (src, dst) in enumerate(((q_hbm, xq), (k_hbm, xk), (v_hbm, xv), (gain_hbm, gain_ref)))
    ]
    for load in loads:
        load.start()

    barrier = pltpu.get_barrier_semaphore()
    peers = [chip(d) for d in PEERS] + [sibling] + [at_y(d) for d in range(1, NY)]
    for peer in peers:
        pl.semaphore_signal(barrier, inc=1, device_id=peer, device_id_type=MESH)

    def means(src, dst):
        for j in range(TOKENS // SEGMENT):
            rows = src[pl.ds(j * 2 * SEGMENT, 2 * SEGMENT), :].astype(F32)
            total = jnp.sum(rows.reshape(2 * SEGMENT // 8, 8, DIM), axis=0)
            total = total + pltpu.roll(total, 4, 0)
            total = total + pltpu.roll(total, 2, 0)
            marks[j : j + 1, :] = total[0:1]
            marks[8 + j : 9 + j, :] = total[1:2]
        dst[c, x, z] = (marks[...] * (1.0 / SEGMENT)).astype(BF16)

    def spread(block):
        return [send_all([(block, block, d) for d in PEERS], rparts)]

    def head_rows(src, dst):
        def body(j, _):
            wide[0:512, :] = src[pl.ds(j * 512, 512), :].astype(F32)
            for h in range(2):
                dst[h, pl.ds(j * 256, 256), :] = wide[pl.ds(h, 256, stride=2), :].astype(BF16)
            return 0

        lax.fori_loop(0, TOKENS // 256, body, 0)

    def landmarks(g, m, core):
        rows = g[core].astype(F32).reshape(NX * NZ, 16, DIM)
        for h in range(2):
            m[h, core] = rows[:, 8 * h : 8 * h + 8, :].reshape(MARKS // 2, DIM).astype(BF16)

    loads[0].wait()
    means(xq, gq)
    pl.semaphore_wait(barrier, len(peers))
    q_copies = spread(gq.at[c, x, z])
    loads[1].wait()
    means(xk, gk)
    k_copies = spread(gk.at[c, x, z])
    head_rows(xk, kh)
    loads[2].wait()
    loads[3].wait()
    head_rows(xv, vh)
    head_rows(xq, qh)
    arrived(q_copies)
    q_copies = [send(gq.at[c], gq.at[c], sibling)]
    landmarks(gq, mq, c)

    def local_part(h, rows):
        scores = dot(rows, kh[h], NT)
        top = jnp.max(scores, axis=1, keepdims=True)
        weights = jnp.exp2((scores - top) * SCALE2)
        total = jnp.sum(weights, axis=1, keepdims=True)
        part = dot(weights.astype(BF16), vh[h]) * (1.0 / total)
        return part, jnp.broadcast_to(top * SCALE2 + jnp.log2(total), part.shape)

    core_copies = []

    def part_away(half):
        away[half, 0], away[half, 1] = local_part(other, mq[other, half])
        core_copies.append(send(away.at[half], rcore.at[half], sibling))

    part_away(c)
    arrived(q_copies)
    landmarks(gq, mq, other)
    part_away(other)
    arrived(k_copies)
    k_copies = [send(gk.at[c], gk.at[c], sibling)]
    value, log_sum = local_part(c, mq[c].reshape(MARKS, DIM))
    arrived(core_copies)
    far = jnp.concatenate([rcore[0, 0], rcore[1, 0]], axis=0)
    far_log = jnp.concatenate([rcore[0, 1], rcore[1, 1]], axis=0)
    top = jnp.maximum(log_sum, far_log)
    near_weight, far_weight = jnp.exp2(log_sum - top), jnp.exp2(far_log - top)
    total = near_weight + far_weight
    value = (value * near_weight + far * far_weight) * (1.0 / total)
    log_sum = top + jnp.log2(total)
    for i in range(NX):
        cut = slice(128 * i, 128 * i + 128)
        parts[i] = value[cut].T.astype(BF16).reshape(NZ, 16, DIM)
        logs[i] = log_sum[cut].T[0:1]
    log_pieces = [(logs.at[at(d)[1]], rlogs.at[n], d) for n, d in enumerate(PEERS)]
    part_pieces = [(parts.at[at(d)[1], at(d)[0]], rparts.at[n], d) for n, d in enumerate(PEERS)]
    reduce_copies = [send_all(log_pieces, rlogs), send_all(part_pieces, rparts)]

    arrived(k_copies)
    for core in range(2):
        landmarks(gk, mk, core)
    scores = dot(mq[c].reshape(MARKS, DIM), mk[c].reshape(MARKS, DIM), NT)
    weights = jnp.exp2((scores - jnp.max(scores, axis=1, keepdims=True)) * SCALE2)
    a = weights * (1.0 / jnp.sum(weights, axis=1, keepdims=True))
    magnitude = jnp.abs(a)
    column_top = jnp.max(jnp.sum(magnitude, axis=0, keepdims=True), axis=1, keepdims=True)
    row_top = jnp.max(jnp.sum(magnitude, axis=1, keepdims=True), axis=0, keepdims=True)
    shrink = 1.0 / (column_top * row_top)

    def eye_times(f):
        i = lax.broadcasted_iota(jnp.int32, (MARKS, MARKS), 0)
        j = lax.broadcasted_iota(jnp.int32, (MARKS, MARKS), 1)
        return jnp.where(i == j, F32(f), F32(0.0))

    a2 = split(a)
    t0[...] = dot3(a2, a2, NT) * shrink
    p0 = split(t0[...])
    t1[...] = dot3(p0, p0)
    cube = dot(t1[...].astype(BF16), p0[0])
    w_ref[...] = eye_times(13.0) - 15.0 * t0[...] + 7.0 * t1[...] - cube
    t2[...] = 0.25 * dot3(p0, split(w_ref[...]))

    arrived(reduce_copies)
    own_log, far_logs = logs[x], rlogs[...]
    top = jnp.maximum(own_log, jnp.max(far_logs, axis=0))
    own_weight, far_weights = jnp.exp2(own_log - top), jnp.exp2(far_logs - top[None])
    total = own_weight + jnp.sum(far_weights, axis=0)
    value = parts[x, z].astype(F32) * own_weight + jnp.sum(rparts[...].astype(F32) * far_weights, axis=0)
    kvt[x, z] = (value * (1.0 / total)).astype(BF16)
    kv_copies = spread(kvt.at[x, z])

    p1 = split(t2[...])
    t0[...] = dot3(p1, p1)
    cube = dot(t0[...].astype(BF16), p1[0])
    t1[...] = eye_times(13.0) - 15.0 * t2[...] + 7.0 * t0[...] - cube
    w_ref[...] = dot3(split(w_ref[...]), split(t1[...])) * (shrink * 0.0625)

    def query_weights(h, _):
        scores = dot(mk[h].reshape(MARKS, DIM), qh[h], NT)
        weights = jnp.exp2((scores - jnp.max(scores, axis=0, keepdims=True)) * SCALE2)
        totals[h] = jnp.sum(weights, axis=0, keepdims=True)
        weights_f[h] = weights.astype(BF16)
        return 0

    lax.fori_loop(0, 2, query_weights, 0)

    arrived(kv_copies)
    for i in range(NX):
        kvf[:, 128 * i : 128 * i + 128] = kvt[i].reshape(DIM, DIM)
    w2 = split(w_ref[...])
    blended = dot(kvf[...], w2[0]) + dot(kvf[...], w2[1])
    mixt[c] = dot3(split(blended), a2).astype(BF16)
    mix_copy = send(mixt.at[c], mixt.at[c], sibling)

    def attend(h):
        value = dot(mixt[h], weights_f[h]) * (1.0 / totals[h])
        attt[h] = value
        return jnp.sum(value * value, axis=0, keepdims=True)

    squares = attend(c)
    arrived([mix_copy])
    squares = squares + attend(other)
    for n in range(TOKENS // 128):
        sqs[n : n + 1, :] = squares[:, 128 * n : 128 * n + 128]
    y_copies = [send(sqs, sqr.at[d - 1], at_y(d)) for d in (2, 1, 3)]
    for n in range(TOKENS // 128):
        for h in range(2):
            att[h, pl.ds(n * 128, 128), :] = attt[h, :, 128 * n : 128 * n + 128].T * gain_ref[h : h + 1, :]
    arrived(y_copies)
    total = sqs[...] + sqr[0] + sqr[1] + sqr[2]
    factors[...] = lax.rsqrt(total * (1.0 / (8 * DIM)) + EPSILON)
    for copy in started:
        copy.wait_send()


def finish(att, factors, o_hbm, wide, out, out_sem):
    steps = 4
    tokens = TOKENS // steps
    stores = []
    for n in range(steps):
        for i in range(n * tokens // DIM, (n + 1) * tokens // DIM):
            factor = jnp.broadcast_to(factors[i : i + 1, :], (DIM, DIM)).T
            for h in range(2):
                wide[pl.ds(2 * DIM * i + h, DIM, stride=2), :] = att[h, pl.ds(DIM * i, DIM), :] * factor
        cut = pl.ds(n * 2 * tokens, 2 * tokens)
        out[cut, :] = wide[cut, :].astype(BF16)
        stores.append(pltpu.make_async_copy(out.at[cut], o_hbm.at[cut], out_sem.at[n]))
        stores[n].start()
    for store in stores:
        store.wait()


def on_device(queries, key_rows, values, gain):
    rows = 2 * TOKENS
    args = [a.reshape(rows, DIM) for a in (queries, key_rows, values)] + [gain]
    args = [pltpu.with_memory_space_constraint(a, pltpu.HBM) for a in args]
    vmem = pltpu.VMEM
    att, factors = pl.pallas_call(
        kernel,
        out_shape=(jax.ShapeDtypeStruct((2, TOKENS, DIM), F32), jax.ShapeDtypeStruct((16, DIM), F32)),
        in_specs=[pl.BlockSpec(memory_space=pltpu.HBM)] * 4,
        out_specs=(pl.BlockSpec(memory_space=pltpu.VMEM), pl.BlockSpec(memory_space=pltpu.VMEM)),
        scratch_shapes=[
            vmem((rows, DIM), BF16),
            vmem((rows, DIM), BF16),
            vmem((rows, DIM), BF16),
            vmem((2, DIM), F32),
            vmem((2, TOKENS, DIM), BF16),
            vmem((2, TOKENS, DIM), BF16),
            vmem((2, TOKENS, DIM), BF16),
            vmem((16, DIM), F32),
            vmem((NC, NX, NZ, 16, DIM), BF16),
            vmem((NC, NX, NZ, 16, DIM), BF16),
            vmem((2, 2, MARKS // 2, DIM), BF16),
            vmem((2, 2, MARKS // 2, DIM), BF16),
            vmem((512, DIM), F32),
            vmem((2, 2, MARKS // 2, DIM), F32),
            vmem((2, 2, MARKS // 2, DIM), F32),
            vmem((NX, NZ, 16, DIM), BF16),
            vmem((NX, 1, DIM), F32),
            vmem((NP, 16, DIM), BF16),
            vmem((NP, 1, DIM), F32),
            vmem((NX, NZ, 16, DIM), BF16),
            vmem((DIM, MARKS), BF16),
            vmem((2, MARKS, TOKENS), BF16),
            vmem((2, 1, TOKENS), F32),
            vmem((MARKS, MARKS), F32),
            vmem((MARKS, MARKS), F32),
            vmem((MARKS, MARKS), F32),
            vmem((MARKS, MARKS), F32),
            vmem((2, DIM, MARKS), BF16),
            vmem((2, DIM, TOKENS), F32),
            vmem((16, DIM), F32),
            vmem((NY - 1, 16, DIM), F32),
            pltpu.SemaphoreType.DMA((4,)),
            pltpu.SemaphoreType.DMA((13,)),
            pltpu.SemaphoreType.DMA((13,)),
        ],
        compiler_params=pltpu.CompilerParams(
            collective_id=0, has_side_effects=True, vmem_limit_bytes=40 * 1024 * 1024
        ),
    )(*args)
    out = pl.pallas_call(
        finish,
        out_shape=jax.ShapeDtypeStruct((rows, DIM), BF16),
        in_specs=[pl.BlockSpec(memory_space=pltpu.VMEM)] * 2,
        out_specs=pl.BlockSpec(memory_space=pl.ANY),
        scratch_shapes=[
            vmem((rows, DIM), F32),
            vmem((rows, DIM), BF16),
            pltpu.SemaphoreType.DMA((4,)),
        ],
        compiler_params=pltpu.CompilerParams(vmem_limit_bytes=16 * 1024 * 1024),
    )(att, factors)
    return out.reshape(TOKENS, 2, DIM)


def solution(mesh):
    spec = P("seq", "head", None)
    return jax.shard_map(
        on_device,
        mesh=mesh,
        in_specs=(spec, spec, spec, P("head", None)),
        out_specs=spec,
        check_vma=False,
    )
```

```python
import jax
import jax.numpy as jnp
from jax import lax
from jax.experimental import pallas as pl
from jax.experimental.pallas import tpu as pltpu
from jax.sharding import PartitionSpec as P

MESH = pl.DeviceIdType.MESH
F32 = jnp.float32
BF16 = jnp.bfloat16
NZ, NX, NC, NY = 8, 4, 2, 4
TOKENS = 2048
DIM = 128
MARKS = 512
SEGMENT = 256
EPSILON = 1e-06
LOG2E = 1.4426950408889634
SCALE2 = DIM ** (-0.5) * LOG2E

NN = (((1,), (0,)), ((), ()))
NT = (((1,), (1,)), ((), ()))


def dot(a, b, dims=NN):
    return lax.dot_general(a, b, dims, preferred_element_type=F32)


def split(a):
    high = a.astype(BF16)
    return high, (a - high.astype(F32)).astype(BF16)


def dot3(a, b, dims=NN):
    return dot(a[0], b[0], dims) + (dot(a[0], b[1], dims) + dot(a[1], b[0], dims))


PEERS = sorted(
    ((dz, dx) for dz in range(NZ) for dx in range(NX) if dz or dx),
    key=lambda p: -(min(p[0], NZ - p[0]) + min(p[1], NX - p[1])),
)
NP = len(PEERS)


def kernel(
    q_hbm, k_hbm, v_hbm, gain_hbm, att, factors,
    xq, xk, xv, gain_ref, qh, kh, vh, marks, gq, gk, mq, mk, wide,
    away, rcore, parts, logs, rparts, rlogs, kvt, kvf, weights_f, totals,
    t0, t1, t2, w_ref, mixt, attt, sqs, sqr,
    local_sem, ssem, rsem,
):
    s = lax.axis_index("seq")
    y = lax.axis_index("head")
    c = lax.rem(s, 2)
    x = lax.rem(lax.div(s, 2), NX)
    z = lax.div(s, 2 * NX)
    other = 1 - c

    def at(d):
        return lax.rem(z + d[0], NZ), lax.rem(x + d[1], NX)

    def chip(d):
        zz, xx = at(d)
        return {"seq": (zz * NX + xx) * 2 + c}

    sibling = {"seq": (z * NX + x) * 2 + other}

    def at_y(d):
        return {"head": lax.rem(y + d, NY)}

    started = []

    def remote(src, dst, target, n):
        return pltpu.make_async_remote_copy(
            src_ref=src, dst_ref=dst, send_sem=ssem.at[n], recv_sem=rsem.at[n],
            device_id=target, device_id_type=MESH,
        )

    def send(src, dst, target):
        copy = remote(src, dst, target, len(started))
        copy.start()
        started.append(copy)
        return copy

    def send_all(pieces, size_of):
        n = len(started)
        for src, dst, d in pieces:
            remote(src, dst, chip(d), n).start()
        started.append(remote(size_of, size_of, sibling, n))
        return started[n]

    def arrived(copies):
        for copy in copies:
            copy.wait_recv()

    loads = [
        pltpu.make_async_copy(src, dst, local_sem.at[i])
        for i, (src, dst) in enumerate(((q_hbm, xq), (k_hbm, xk), (v_hbm, xv), (gain_hbm, gain_ref)))
    ]
    barrier = pltpu.get_barrier_semaphore()
    peers = [chip(d) for d in PEERS] + [sibling] + [at_y(d) for d in range(1, NY)]
    for peer in peers:
        pl.semaphore_signal(barrier, inc=1, device_id=peer, device_id_type=MESH)
    for load in loads:
        load.start()

    def means(src, dst):
        for j in range(TOKENS // SEGMENT):
            rows = src[pl.ds(j * 2 * SEGMENT, 2 * SEGMENT), :].astype(F32)
            total = jnp.sum(rows.reshape(2 * SEGMENT // 8, 8, DIM), axis=0)
            total = total + pltpu.roll(total, 4, 0)
            total = total + pltpu.roll(total, 2, 0)
            marks[j : j + 1, :] = total[0:1]
            marks[8 + j : 9 + j, :] = total[1:2]
        dst[c, x, z] = (marks[...] * (1.0 / SEGMENT)).astype(BF16)

    def spread(block):
        return [send_all([(block, block, d) for d in PEERS], rparts)]

    def head_rows(src, dst):
        def body(j, _):
            wide[0:512, :] = src[pl.ds(j * 512, 512), :].astype(F32)
            for h in range(2):
                dst[h, pl.ds(j * 256, 256), :] = wide[pl.ds(h, 256, stride=2), :].astype(BF16)
            return 0

        lax.fori_loop(0, TOKENS // 256, body, 0)

    def landmarks(g, m, core):
        rows = g[core].astype(F32).reshape(NX * NZ, 16, DIM)
        for h in range(2):
            m[h, core] = rows[:, 8 * h : 8 * h + 8, :].reshape(MARKS // 2, DIM).astype(BF16)

    loads[0].wait()
    means(xq, gq)
    pl.semaphore_wait(barrier, len(peers))
    q_copies = spread(gq.at[c, x, z])
    loads[1].wait()
    means(xk, gk)
    block = gk.at[c, x, z]
    k_copies = [send_all([(block, block, (d, 0)) for d in (4, 3, 5, 2, 6, 1, 7)], rparts.at[pl.ds(0, NZ - 1)])]
    head_rows(xk, kh)
    loads[2].wait()
    loads[3].wait()
    head_rows(xv, vh)
    head_rows(xq, qh)
    arrived(q_copies)
    q_copies = [send(gq.at[c], gq.at[c], sibling)]
    arrived(k_copies)
    column = gk.at[c, x]
    k_copies = [send_all([(column, column, (0, d)) for d in (2, 1, 3)], rparts.at[pl.ds(0, (NX - 1) * NZ)])]
    landmarks(gq, mq, c)

    def local_part(h, rows):
        scores = dot(rows, kh[h], NT)
        top = jnp.max(scores, axis=1, keepdims=True)
        weights = jnp.exp2((scores - top) * SCALE2)
        total = jnp.sum(weights, axis=1, keepdims=True)
        part = dot(weights.astype(BF16), vh[h]) * (1.0 / total)
        return part, jnp.broadcast_to(top * SCALE2 + jnp.log2(total), part.shape)

    core_copies = []

    def part_away(half):
        away[half, 0], away[half, 1] = local_part(other, mq[other, half])
        core_copies.append(send(away.at[half], rcore.at[half], sibling))

    part_away(c)
    arrived(q_copies)
    landmarks(gq, mq, other)
    part_away(other)
    value, log_sum = local_part(c, mq[c].reshape(MARKS, DIM))
    arrived(k_copies)
    k_copies = [send(gk.at[c], gk.at[c], sibling)]
    arrived(core_copies)
    far = jnp.concatenate([rcore[0, 0], rcore[1, 0]], axis=0)
    far_log = jnp.concatenate([rcore[0, 1], rcore[1, 1]], axis=0)
    top = jnp.maximum(log_sum, far_log)
    near_weight, far_weight = jnp.exp2(log_sum - top), jnp.exp2(far_log - top)
    total = near_weight + far_weight
    value = (value * near_weight + far * far_weight) * (1.0 / total)
    log_sum = top + jnp.log2(total)
    for i in range(NX):
        cut = slice(128 * i, 128 * i + 128)
        parts[i] = value[cut].T.astype(BF16).reshape(NZ, 16, DIM)
        logs[i] = log_sum[cut].T[0:1]
    log_pieces = [(logs.at[at(d)[1]], rlogs.at[n], d) for n, d in enumerate(PEERS)]
    part_pieces = [(parts.at[at(d)[1], at(d)[0]], rparts.at[n], d) for n, d in enumerate(PEERS)]
    reduce_copies = [send_all(log_pieces, rlogs), send_all(part_pieces, rparts)]

    arrived(k_copies)
    for core in range(2):
        landmarks(gk, mk, core)
    scores = dot(mq[c].reshape(MARKS, DIM), mk[c].reshape(MARKS, DIM), NT)
    weights = jnp.exp2((scores - jnp.max(scores, axis=1, keepdims=True)) * SCALE2)
    a = weights * (1.0 / jnp.sum(weights, axis=1, keepdims=True))
    magnitude = jnp.abs(a)
    column_top = jnp.max(jnp.sum(magnitude, axis=0, keepdims=True), axis=1, keepdims=True)
    row_top = jnp.max(jnp.sum(magnitude, axis=1, keepdims=True), axis=0, keepdims=True)
    shrink = 1.0 / (column_top * row_top)

    def eye_times(f):
        i = lax.broadcasted_iota(jnp.int32, (MARKS, MARKS), 0)
        j = lax.broadcasted_iota(jnp.int32, (MARKS, MARKS), 1)
        return jnp.where(i == j, F32(f), F32(0.0))

    a2 = split(a)
    t0[...] = dot3(a2, a2, NT) * shrink
    p0 = split(t0[...])
    t1[...] = dot3(p0, p0)
    cube = dot(t1[...].astype(BF16), p0[0])
    w_ref[...] = eye_times(13.0) - 15.0 * t0[...] + 7.0 * t1[...] - cube
    t2[...] = 0.25 * dot3(p0, split(w_ref[...]))

    arrived(reduce_copies)
    own_log, far_logs = logs[x], rlogs[...]
    top = jnp.maximum(own_log, jnp.max(far_logs, axis=0))
    own_weight, far_weights = jnp.exp2(own_log - top), jnp.exp2(far_logs - top[None])
    total = own_weight + jnp.sum(far_weights, axis=0)
    value = parts[x, z].astype(F32) * own_weight + jnp.sum(rparts[...].astype(F32) * far_weights, axis=0)
    kvt[x, z] = (value * (1.0 / total)).astype(BF16)
    kv_copies = spread(kvt.at[x, z])

    p1 = split(t2[...])
    t0[...] = dot3(p1, p1)
    cube = dot(t0[...].astype(BF16), p1[0])
    t1[...] = eye_times(13.0) - 15.0 * t2[...] + 7.0 * t0[...] - cube
    w_ref[...] = dot3(split(w_ref[...]), split(t1[...])) * (shrink * 0.0625)

    def query_weights(h, _):
        scores = dot(mk[h].reshape(MARKS, DIM), qh[h], NT)
        weights = jnp.exp2((scores - jnp.max(scores, axis=0, keepdims=True)) * SCALE2)
        totals[h] = jnp.sum(weights, axis=0, keepdims=True)
        weights_f[h] = weights.astype(BF16)
        return 0

    lax.fori_loop(0, 2, query_weights, 0)

    arrived(kv_copies)
    for i in range(NX):
        kvf[:, 128 * i : 128 * i + 128] = kvt[i].reshape(DIM, DIM)
    w2 = split(w_ref[...])
    blended = dot(kvf[...], w2[0]) + dot(kvf[...], w2[1])
    mixt[c] = dot3(split(blended), a2).astype(BF16)
    mix_copy = send(mixt.at[c], mixt.at[c], sibling)

    def attend(h):
        value = dot(mixt[h], weights_f[h]) * (1.0 / totals[h])
        attt[h] = value
        return jnp.sum(value * value, axis=0, keepdims=True)

    squares = attend(c)
    arrived([mix_copy])
    squares = squares + attend(other)
    for n in range(TOKENS // 128):
        sqs[n : n + 1, :] = squares[:, 128 * n : 128 * n + 128]
    y_copies = [send(sqs, sqr.at[d - 1], at_y(d)) for d in (2, 1, 3)]
    for n in range(TOKENS // 128):
        for h in range(2):
            att[h, pl.ds(n * 128, 128), :] = attt[h, :, 128 * n : 128 * n + 128].T * gain_ref[h : h + 1, :]
    arrived(y_copies)
    total = sqs[...] + sqr[0] + sqr[1] + sqr[2]
    factors[...] = lax.rsqrt(total * (1.0 / (8 * DIM)) + EPSILON)
    for copy in started:
        copy.wait_send()


def finish(att, factors, o_hbm, wide, out, out_sem):
    steps = 4
    tokens = TOKENS // steps
    stores = []
    for n in range(steps):
        for i in range(n * tokens // DIM, (n + 1) * tokens // DIM):
            factor = jnp.broadcast_to(factors[i : i + 1, :], (DIM, DIM)).T
            for h in range(2):
                wide[pl.ds(2 * DIM * i + h, DIM, stride=2), :] = att[h, pl.ds(DIM * i, DIM), :] * factor
        cut = pl.ds(n * 2 * tokens, 2 * tokens)
        out[cut, :] = wide[cut, :].astype(BF16)
        stores.append(pltpu.make_async_copy(out.at[cut], o_hbm.at[cut], out_sem.at[n]))
        stores[n].start()
    for store in stores:
        store.wait()


def on_device(queries, key_rows, values, gain):
    rows = 2 * TOKENS
    args = [a.reshape(rows, DIM) for a in (queries, key_rows, values)] + [gain]
    args = [pltpu.with_memory_space_constraint(a, pltpu.HBM) for a in args]
    vmem = pltpu.VMEM
    att, factors = pl.pallas_call(
        kernel,
        out_shape=(jax.ShapeDtypeStruct((2, TOKENS, DIM), F32), jax.ShapeDtypeStruct((16, DIM), F32)),
        in_specs=[pl.BlockSpec(memory_space=pltpu.HBM)] * 4,
        out_specs=(pl.BlockSpec(memory_space=pltpu.VMEM), pl.BlockSpec(memory_space=pltpu.VMEM)),
        scratch_shapes=[
            vmem((rows, DIM), BF16),
            vmem((rows, DIM), BF16),
            vmem((rows, DIM), BF16),
            vmem((2, DIM), F32),
            vmem((2, TOKENS, DIM), BF16),
            vmem((2, TOKENS, DIM), BF16),
            vmem((2, TOKENS, DIM), BF16),
            vmem((16, DIM), F32),
            vmem((NC, NX, NZ, 16, DIM), BF16),
            vmem((NC, NX, NZ, 16, DIM), BF16),
            vmem((2, 2, MARKS // 2, DIM), BF16),
            vmem((2, 2, MARKS // 2, DIM), BF16),
            vmem((520, DIM), F32),
            vmem((2, 2, MARKS // 2, DIM), F32),
            vmem((2, 2, MARKS // 2, DIM), F32),
            vmem((NX, NZ, 16, DIM), BF16),
            vmem((NX, 1, DIM), F32),
            vmem((NP, 16, DIM), BF16),
            vmem((NP, 1, DIM), F32),
            vmem((NX, NZ, 16, DIM), BF16),
            vmem((DIM, MARKS), BF16),
            vmem((2, MARKS, TOKENS), BF16),
            vmem((2, 1, TOKENS), F32),
            vmem((MARKS, MARKS), F32),
            vmem((MARKS, MARKS), F32),
            vmem((MARKS, MARKS), F32),
            vmem((MARKS, MARKS), F32),
            vmem((2, DIM, MARKS), BF16),
            vmem((2, DIM, TOKENS), F32),
            vmem((16, DIM), F32),
            vmem((NY - 1, 16, DIM), F32),
            pltpu.SemaphoreType.DMA((4,)),
            pltpu.SemaphoreType.DMA((14,)),
            pltpu.SemaphoreType.DMA((14,)),
        ],
        compiler_params=pltpu.CompilerParams(
            collective_id=0, has_side_effects=True, vmem_limit_bytes=40 * 1024 * 1024
        ),
    )(*args)
    out = pl.pallas_call(
        finish,
        out_shape=jax.ShapeDtypeStruct((rows, DIM), BF16),
        in_specs=[pl.BlockSpec(memory_space=pltpu.VMEM)] * 2,
        out_specs=pl.BlockSpec(memory_space=pl.ANY),
        scratch_shapes=[
            vmem((rows + 8, DIM), F32),
            vmem((rows, DIM), BF16),
            pltpu.SemaphoreType.DMA((4,)),
        ],
        compiler_params=pltpu.CompilerParams(vmem_limit_bytes=16 * 1024 * 1024),
    )(att, factors)
    return out.reshape(TOKENS, 2, DIM)


def solution(mesh):
    spec = P("seq", "head", None)
    return jax.shard_map(
        on_device,
        mesh=mesh,
        in_specs=(spec, spec, spec, P("head", None)),
        out_specs=spec,
        check_vma=False,
    )
```
